256 devices in a mesh: doc: 32 (over x, z), cent: 8 (over y, core).
Axes of the slice: x: 4, y: 4, z: 8, core: 2. Of those that a mesh axis runs over, the one named last changes fastest.
Arguments:
- embeddings: float32 [65536, 1024], P('doc', 'cent'), may hold values from -320 to 320
- row_mask: int32 [65536], P('doc'), may hold values from 0 to 1, as said below
- block_cluster: int32 [512], P('doc'), may hold values from 0 to 100351, as said below
- candidates: int32 [65536, 8], P('doc'), may hold values from 0 to 100351, as said below
- old_centroids: float32 [100352, 1024], P('doc', 'cent'), may hold values from -0.1875 to 0.1875
Outputs:
- member_sums: float32 [100352, 1024], P('doc', 'cent')
- member_counts: int32 [100352], P('doc')
- centroids: float32 [100352, 1024], P('doc', 'cent')
- cosines: float32 [65536, 8], P(('doc', 'cent'))
The draws below stay inside these ranges and needn't reach their ends.
Inputs may be any that keep to these rules, and one draw needn't show every extreme that they name: `row_mask`: in each block of 128 rows the live rows come first, at least one; the first block of each 2048 rows is full. `block_cluster`: within the blocks of one index of doc the values never fall. Those blocks name centroids of the range c * 3136 to c * 3136 + 3135 in at most 2 blocks, for every c; in every draw some range is named in exactly 2 blocks of every index of doc. `candidates`: of the 16384 ids of the rows of one index of doc, exactly 512 lie in each range c * 3136 to c * 3136 + 3135.
All inputs are finite; a program needn't handle non-finite values.
Results may differ from the reference program's by a relative error of at most 0.0003.
Values sent between devices are 32-bit elements; how exact they have to be, the bound alone decides.
A program may use at most 128 MiB of HBM per device.

```python
import math
import jax
import jax.numpy as jnp
from jax import lax

D = 1024
BLOCK = 128
CAND = 8
KD = 3136
R_DEV = 2048
ROWS = 65536
K = 100352
BLOCKS = 512
CAPB = 2


def draw_embeddings(key, part):
    key = jax.random.fold_in(key, 11)
    key_base, key_cols, key_rows = jax.random.split(key, 3)
    rising = 1.0 + 2.0 * jnp.arange(D, dtype=jnp.float32) / (D - 1)
    columns = rising * jnp.exp(jax.random.uniform(key_cols, (D,), jnp.float32, -0.7, 0.7))
    base = jnp.clip(jax.random.normal(key_base, (ROWS, D), jnp.float32), -5.0, 5.0)
    scales = jnp.exp(jax.random.uniform(key_rows, (ROWS, 1), jnp.float32, 0.0, math.log(10.0)))
    return base * scales * columns[None, :]


def draw_row_mask(key, part):
    key = jax.random.fold_in(key, 12)
    lengths = jax.random.randint(key, (BLOCKS,), 1, BLOCK + 1)
    first_block = jnp.arange(BLOCKS) % (R_DEV // BLOCK) == 0
    lengths = jnp.where(first_block, BLOCK, lengths)
    position = jnp.arange(ROWS) % BLOCK
    return (position < jnp.repeat(lengths, BLOCK)).astype(jnp.int32)


def draw_block_cluster(key, part):
    key = jax.random.fold_in(key, 13)
    devices = ROWS // R_DEV
    per_device = R_DEV // BLOCK
    key_hot, key_devices = jax.random.split(key)
    hottest = jax.random.randint(key_hot, (), 0, devices)

    def one_device(dev_key):
        key_perm, key_local = jax.random.split(dev_key)
        slot_range = jnp.arange((devices - 1) * CAPB)
        others = (hottest + 1 + slot_range // CAPB) % devices
        picked = jax.random.permutation(key_perm, others)[:per_device - CAPB]
        owners_all = jnp.concatenate([jnp.full((CAPB,), hottest, jnp.int32), picked.astype(jnp.int32)])
        local_ids = jax.random.randint(key_local, (per_device,), 0, KD)
        return jnp.sort(owners_all * KD + local_ids)
    return jax.vmap(one_device)(jax.random.split(key_devices, devices)).reshape(BLOCKS).astype(jnp.int32)


def draw_candidates(key, part):
    key = jax.random.fold_in(key, 14)
    devices = ROWS // R_DEV
    requests = CAND * R_DEV

    def one_device(dev_key):
        key_perm, key_local = jax.random.split(dev_key)
        owners_all = jax.random.permutation(key_perm, jnp.arange(requests)) % devices
        local_ids = jax.random.randint(key_local, (requests,), 0, KD)
        return owners_all * KD + local_ids
    return jax.vmap(one_device)(jax.random.split(key, devices)).reshape(ROWS, CAND).astype(jnp.int32)


def shard_levels(key, dims, shards, least, largest):
    def one(dim, blocks):
        steps = jax.random.uniform(jax.random.fold_in(jax.random.fold_in(key, 6), dim), (blocks,), jnp.float32, least / len(shards), largest / len(shards))
        return jnp.repeat(jnp.exp(steps), dims[dim] // blocks).reshape((-1,) + (1,) * (len(dims) - dim - 1))

    factor_of = one(*shards[0])
    for cut in shards[1:]:
        factor_of = factor_of * one(*cut)
    return factor_of


def scatter_about(rng, extent, width, limit, cuts=(), kind=jnp.bfloat16):
    level = shard_levels(rng, extent, cuts, -0.22, 0.18) if cuts else 1.0
    values = jax.random.normal(rng, extent, jnp.float32) * width * level
    return jnp.minimum(jnp.maximum(values, -limit), limit).astype(kind)


def setup_inputs(seed: int = 0) -> dict:
    key_of = jax.random.split(jax.random.key(seed), 6)
    embeddings = draw_embeddings(jax.random.fold_in(key_of[5], 71), 0)
    row_mask = draw_row_mask(jax.random.fold_in(key_of[5], 71), 0)
    block_cluster = draw_block_cluster(jax.random.fold_in(key_of[5], 71), 0)
    candidates = draw_candidates(jax.random.fold_in(key_of[5], 71), 0)
    old_centroids = scatter_about(key_of[4], (K, D), (D ** -0.5), 0.1875, ((0, 32), (1, 8)), jnp.float32)
    return {"embeddings": embeddings, "row_mask": row_mask, "block_cluster": block_cluster, "candidates": candidates, "old_centroids": old_centroids}


def reference(embeddings, row_mask, block_cluster, candidates, old_centroids):
    squares = lax.optimization_barrier(jnp.sum(embeddings * embeddings, axis=1))
    unit_rows = embeddings * lax.rsqrt(squares + 1e-06)[:, None]
    live_rows = row_mask.astype(jnp.float32)
    masked = unit_rows * live_rows[:, None]
    block_sums = lax.optimization_barrier(jnp.sum(masked.reshape(-1, BLOCK, D), axis=1))
    block_counts = lax.optimization_barrier(jnp.sum(live_rows.reshape(-1, BLOCK), axis=1))
    member_sums = jax.ops.segment_sum(block_sums, block_cluster, num_segments=K)
    counts = jax.ops.segment_sum(block_counts, block_cluster, num_segments=K)
    cent_squares = lax.optimization_barrier(jnp.sum(member_sums * member_sums, axis=1))
    centroids = jnp.where(counts[:, None] > 0, member_sums * lax.rsqrt(cent_squares + 1e-06)[:, None], old_centroids)
    groups = ROWS // R_DEV

    def cosine_group(pieces):
        unit_part, cand_part, live_part = pieces
        picked = centroids[cand_part]
        return lax.optimization_barrier(jnp.sum(picked * unit_part[:, None, :], axis=-1)) * live_part[:, None]
    cosines = lax.map(cosine_group, (unit_rows.reshape(groups, R_DEV, D), candidates.reshape(groups, R_DEV, CAND), live_rows.reshape(groups, R_DEV)))
    return (member_sums, counts.astype(jnp.int32), centroids, cosines.reshape(ROWS, CAND))
```

```python
import functools

import jax
import jax.numpy as jnp
from jax import lax
from jax.experimental import pallas as pl
from jax.experimental.pallas import tpu as pltpu
from jax.sharding import PartitionSpec as P

MESH = pl.DeviceIdType.MESH
F32, BF16, I32 = jnp.float32, jnp.bfloat16, jnp.int32
Z_CHIPS = 8
LANES = 128
SLOTS = 64
EXACT = lax.Precision.HIGHEST
NT = (((1,), (1,)), ((), ()))


def iota(shape, dim):
    return lax.broadcasted_iota(I32, shape, dim)


def split3(v):
    a = v.astype(BF16)
    rest = v - a.astype(F32)
    b = rest.astype(BF16)
    return a, b, (rest - b.astype(F32)).astype(BF16)


def kernel(
    nd, nz, nc,
    emb, old, live_in, cand, blk,
    ms, cnt, cen, cos,
    dr, dl, dmid, tr, tl, own_tab, tmid, trp, tlp,
    sq_src, sq_buf, scale, bsum, bcnt, pos, loc_hi, loc_lo, hi_ref, lo_ref,
    msgs, rbuf, sq2_src, sq2_buf, rhs, psend, pbuf, lsend, lbuf, srow, sloc,
    stage, part, s1buf, full, tbuf,
    zr_s, zr_r, zl_s, zl_r, xr_s, xr_r, xl_s, xl_r,
    sq_s, sq_r, sq2_s, sq2_r, a2a_s, a2a_r, p_s, p_r, l_s, l_r, sm_sem, s1_s, s1_r, t_s, t_r,
):
    nx = nd // nz
    rows, owned = emb.shape[0], old.shape[0]
    blocks = blk.shape[0]
    me = lax.axis_index("doc")
    c = lax.axis_index("cent")
    x, z = me // nz, me % nz
    per_z = pos.shape[0] * LANES // nz
    lrows = per_z // LANES
    per_owner = per_z // nx
    urows = lrows // nx

    def copy(src, dst, ssem, rsem, doc, cent):
        return pltpu.make_async_remote_copy(
            src_ref=src, dst_ref=dst, send_sem=ssem, recv_sem=rsem,
            device_id=(doc, cent), device_id_type=MESH,
        )

    bar = pltpu.get_barrier_semaphore()

    def greet(doc, cent):
        pl.semaphore_signal(bar, inc=1, device_id=(doc, cent), device_id_type=MESH)

    lax.fori_loop(1, nd, lambda k, _: (greet((me + k) % nd, c), 0)[1], 0)
    lax.fori_loop(1, nc, lambda k, _: (greet(me, (c + k) % nc), 0)[1], 0)

    @pl.when(c != z)
    def _():
        lax.fori_loop(1, nz, lambda k, _: (greet(x * nz + (z + k) % nz, z), 0)[1], 0)
        pl.semaphore_wait(bar, nd - 1 + nc - 1 + nz - 1)

    @pl.when(c == z)
    def _():
        pl.semaphore_wait(bar, nd - 1 + nc - 1)

    def ring(n, own, right, left, mid, rs, rr, ls, lr, right_id, left_id):
        half = own.shape[0] // 2
        last = n // 2
        out_r, out_l = {}, {}
        for s in range(1, last + 1):
            src_r = own if s == 1 else right[s - 2]
            src_l = own if s == 1 else left[s - 2]
            for h in (0, 1):
                cut = pl.ds(h * half, half)
                if s < last or h == 0:
                    dst = (right[s - 1] if s < last else mid).at[cut]
                    out_r[s, h] = copy(src_r.at[cut], dst, rs.at[s - 1, h], rr.at[s - 1, h], right_id, c)
                if s < last or h == 1:
                    dst = (left[s - 1] if s < last else mid).at[cut]
                    out_l[s, h] = copy(src_l.at[cut], dst, ls.at[s - 1, h], lr.at[s - 1, h], left_id, c)
        return out_r, out_l

    zr, zl = ring(nz, emb, dr, dl, dmid, zr_s, zr_r, zl_s, zl_r,
                  x * nz + (z + 1) % nz, x * nz + (z + nz - 1) % nz)
    xr, xl = ring(nx, old, tr, tl, tmid, xr_s, xr_r, xl_s, xl_r,
                  (x + 1) % nx * nz + z, (x + nx - 1) % nx * nz + z)

    def forward(right, left, s, h):
        right[s, h].wait_recv()
        if (s + 1, h) in right:
            right[s + 1, h].start()
        left[s, 1 - h].wait_recv()
        if (s + 1, 1 - h) in left:
            left[s + 1, 1 - h].start()

    zr[1, 0].start()
    zl[1, 1].start()
    xr[1, 0].start()
    xl[1, 1].start()
    zr[1, 1].start()
    zl[1, 0].start()
    xr[1, 1].start()
    xl[1, 0].start()

    def cent_copy(src, buf, ss, rs, k):
        return copy(src, buf.at[c], ss.at[k], rs.at[c], me, (c + k) % nc)

    def cent_start(src, buf, ss, rs):
        lax.fori_loop(1, nc, lambda k, _: (cent_copy(src, buf, ss, rs, k).start(), 0)[1], 0)
        buf[c] = src[...]

    def cent_wait(src, buf, ss, rs):
        def body(k, _):
            other = (c + k) % nc
            copy(src, buf.at[other], ss.at[k], rs.at[other], me, other).wait()
            return 0
        lax.fori_loop(1, nc, body, 0)

    def cross_copy(src, dst, ss, rs, k):
        return copy(src, dst(z), ss.at[k], rs.at[z], x * nz + c, (c + k) % nc)

    def cross_start(src, dst, ss, rs):
        lax.fori_loop(1, nc, lambda k, _: (cross_copy(src, dst, ss, rs, k).start(), 0)[1], 0)

        @pl.when(c != z)
        def _():
            cross_copy(src, dst, ss, rs, 0).start()

        @pl.when(c == z)
        def _():
            dst(z)[...] = src[...]

    def cross_wait(src, dst, ss, rs):
        def body(k, _):
            other = (z + k) % nz
            copy(src, dst(other), ss.at[k], rs.at[other], x * nz + c, (c + k) % nc).wait()
            return 0
        lax.fori_loop(1, nz, body, 0)

        @pl.when(c != z)
        def _():
            cross_copy(src, dst, ss, rs, 0).wait()

    for table in (own_tab, tmid, trp, tlp):
        table[owned:, :] = jnp.zeros((table.shape[0] - owned, LANES), F32)

    def squares(b, _):
        t = emb[pl.ds(pl.multiple_of(b * LANES, LANES), LANES), :].T
        sq_src[pl.ds(b, 1), :] = jnp.sum(t * t, axis=0, keepdims=True)
        return 0

    lax.fori_loop(0, rows // LANES, squares, 0)
    cent_start(sq_src, sq_buf, sq_s, sq_r)

    ids = jnp.concatenate([cand[:, LANES * i:LANES * (i + 1)] for i in range(rows // LANES)], 0).astype(F32)
    qrows = ids.shape[0]
    owner = jnp.floor((ids + 0.5) * (1.0 / owned))
    loc = ids - owner * owned
    loc_top = jnp.floor(loc * (1.0 / LANES))
    loc_hi[...] = loc_top
    loc_lo[...] = loc - loc_top * LANES
    upper = (iota((LANES, LANES), 0) < iota((LANES, LANES), 1)).astype(F32)
    upper_ones = jnp.concatenate([upper, jnp.ones((LANES, LANES), F32)], 1).astype(BF16)
    lower = (iota((qrows, qrows), 0) > iota((qrows, qrows), 1)).astype(F32).astype(BF16)
    pos[...] = jnp.zeros_like(pos)

    def place(m, _):
        mask = (owner == m.astype(F32)).astype(F32)
        counted = jnp.dot(mask.astype(BF16), upper_ones, preferred_element_type=F32)
        above = jnp.dot(lower, counted[:, LANES:].astype(BF16), preferred_element_type=F32)
        base = ((m % nz) * per_z + (m // nz) * per_owner).astype(F32)
        pos[...] += mask * (counted[:, :LANES] + above + base)
        return 0

    lax.fori_loop(0, nd, place, 0)
    top = jnp.floor(pos[...] * (1.0 / LANES))
    hi_ref[...] = top
    lo_ref[...] = pos[...] - top * LANES

    shift = (c * lrows).astype(F32)
    lane_row = iota((1, LANES), 1).astype(F32)

    def lists(i, acc):
        left_parts, right_parts = [], []
        for j in range(8):
            q = pl.ds(i * 8 + j, 1)
            at = (iota((lrows, LANES), 0).astype(F32) == hi_ref[q, :] - shift).astype(F32)
            left_parts.append(jnp.concatenate(
                [at * i.astype(F32), at * lane_row, at * loc_hi[q, :], at * loc_lo[q, :]], 0).astype(BF16))
            right_parts.append(
                (iota((LANES, LANES), 0).astype(F32) == lo_ref[q, :]).astype(F32).astype(BF16))
        return acc + lax.dot_general(
            jnp.concatenate(left_parts, 1), jnp.concatenate(right_parts, 1), NT, preferred_element_type=F32)

    found = lax.fori_loop(0, qrows // 8, lists, jnp.zeros((4 * lrows, LANES), F32))
    lsend[0] = (found[:lrows] * LANES + found[lrows:2 * lrows]).astype(I32)
    lsend[1] = (found[2 * lrows:3 * lrows] * LANES + found[3 * lrows:]).astype(I32)
    lists_at = lambda s: lbuf.at[s]
    cross_start(lsend, lists_at, l_s, l_r)

    cent_wait(sq_src, sq_buf, sq_s, sq_r)
    total = sq_buf[0]
    for k in range(1, nc):
        total = total + sq_buf[k]
    alive = live_in[...].astype(F32)
    scale[...] = lax.rsqrt(total + 1e-6) * alive

    def block_sum(b, acc):
        weight = jnp.where(iota((blocks, LANES), 0) == b, scale[...], 0.0)
        return acc + jnp.dot(weight, emb[pl.ds(pl.multiple_of(b * LANES, LANES), LANES), :],
                             precision=EXACT, preferred_element_type=F32)

    bsum[...] = lax.fori_loop(0, blocks, block_sum, jnp.zeros((blocks, LANES), F32))
    bcnt[...] = jnp.broadcast_to(jnp.sum(alive, axis=1, keepdims=True), (blocks, LANES))
    owners = [blk[b] // owned for b in range(blocks)]
    place_of = [jnp.int32(0)] + [
        jnp.where(owners[b] == owners[b - 1], 1, 0) for b in range(1, blocks)]
    local = [(blk[b] - owners[b] * owned).astype(F32) for b in range(blocks)]

    def message(o, _):
        tile = jnp.zeros((8, LANES), F32)
        line = iota((8, LANES), 0)
        for b in range(blocks):
            at = jnp.where(owners[b] == o, place_of[b], -8)
            tile = jnp.where(line == at, bsum[b:b + 1, :], tile)
            tile = jnp.where(line == at + 2, local[b], tile)
            tile = jnp.where(line == at + 4, bcnt[b:b + 1, :], tile)
        msgs[o] = tile
        return 0

    lax.fori_loop(0, nd, message, 0)

    def a2a_start(k, _):
        to = (me + k) % nd
        copy(msgs.at[to], rbuf.at[me], a2a_s.at[k], a2a_r.at[me], to, c).start()
        return 0

    def a2a_wait(k, _):
        other = (me + k) % nd
        copy(msgs.at[other], rbuf.at[other], a2a_s.at[k], a2a_r.at[other], other, c).wait()
        return 0

    lax.fori_loop(1, nd, a2a_start, 0)
    rbuf[me] = msgs[me]
    forward(zr, zl, 1, 0)
    lax.fori_loop(1, nd, a2a_wait, 0)

    def slots(first, empty):
        return jnp.concatenate(
            [rbuf[:, first, :], rbuf[:, first + 1, :],
             jnp.full((LANES - 2 * nd, LANES), empty, F32)], 0)

    sums, slot_ids, slot_counts = slots(0, 0.0), slots(2, -1.0), slots(4, 0.0)
    slot_ids = jnp.where(slot_counts > 0, slot_ids, -1.0)
    ids_lane = slot_ids.T
    same = jnp.where((slot_ids == ids_lane) & (slot_counts > 0), 1.0, 0.0)
    group = jnp.dot(same, sums, precision=EXACT, preferred_element_type=F32)
    square = group * group
    sq2_src[...] = jnp.broadcast_to(jnp.sum(square.T, axis=0, keepdims=True), (8, LANES))
    cent_start(sq2_src, sq2_buf, sq2_s, sq2_r)

    earlier = jnp.sum(
        jnp.where(iota((LANES, LANES), 0) < iota((LANES, LANES), 1), same, 0.0), axis=0, keepdims=True)
    first_ids = jnp.where(earlier > 0, -1.0, ids_lane[0:1])
    counts_lane = slot_counts.T[0:1]
    ids_top = jnp.floor(ids_lane[0:1] * (1.0 / LANES))
    ids_low = ids_lane[0:1] - ids_top * LANES
    count_left = jnp.where(iota(cnt.shape, 0).astype(F32) == ids_top, counts_lane, 0.0).astype(BF16)
    count_right = (iota((LANES, LANES), 0).astype(F32) == ids_low).astype(F32).astype(BF16)
    cnt[...] = lax.dot_general(count_left, count_right, NT, preferred_element_type=F32).astype(I32)

    cent_wait(sq2_src, sq2_buf, sq2_s, sq2_r)
    total2 = sq2_buf[0]
    for k in range(1, nc):
        total2 = total2 + sq2_buf[k]
    inverse = lax.rsqrt(jnp.broadcast_to(total2[0:1], (LANES, LANES)) + 1e-6).T
    normal = group * inverse
    psend[0:SLOTS, :] = normal[:SLOTS]
    psend[SLOTS:SLOTS + 8, :] = jnp.broadcast_to(first_ids, (8, LANES))

    def patch_copy(k):
        return copy(psend, pbuf.at[k - 1], p_s.at[k - 1], p_r.at[k - 1], (x + k) % nx * nz + z, c)

    for k in range(1, nx):
        patch_copy(k).start()

    ones = jnp.ones((LANES, LANES), BF16)
    rhs[...] = jnp.concatenate([*split3(normal), ones, *split3(group)], 1)
    step = owned // 7

    def picked(i, chosen, width):
        hit = (iota((step, LANES), 0) + i * step).astype(F32) == chosen
        return jnp.dot(hit.astype(F32).astype(BF16), rhs[:, :width], preferred_element_type=F32)

    def patched(out, before):
        new = out[:, :LANES] + out[:, LANES:2 * LANES] + out[:, 2 * LANES:3 * LANES]
        return jnp.where(out[:, 3 * LANES:4 * LANES] > 0, new, before)

    def cut(i):
        return pl.ds(pl.multiple_of(i * step, 8), step)

    def own_table(i, _):
        out = picked(i, first_ids, 7 * LANES)
        ms[cut(i), :] = out[:, 4 * LANES:5 * LANES] + out[:, 5 * LANES:6 * LANES] + out[:, 6 * LANES:]
        new = patched(out, old[cut(i), :])
        cen[cut(i), :] = new
        own_tab[cut(i), :] = new
        return 0

    lax.fori_loop(0, 7, own_table, 0)
    forward(xr, xl, 1, 0)
    forward(zr, zl, 1, 1)

    cross_wait(lsend, lists_at, l_s, l_r)
    order = [0] + [d * s for d in range(1, nz // 2) for s in (-1, 1)] + [nz // 2]
    source = [(z + nz + d) % nz for d in order]
    for i in range(nz):
        here = pl.ds(i * lrows, lrows)
        pltpu.make_async_copy(lbuf.at[source[i], 0], srow.at[here], sm_sem.at[0, i]).start()
        pltpu.make_async_copy(lbuf.at[source[i], 1], sloc.at[here], sm_sem.at[1, i]).start()
    for i in range(nz):
        here = pl.ds(i * lrows, lrows)
        pltpu.make_async_copy(lbuf.at[source[i], 0], srow.at[here], sm_sem.at[0, i]).wait()
        pltpu.make_async_copy(lbuf.at[source[i], 1], sloc.at[here], sm_sem.at[1, i]).wait()

    documents = {0: emb, nz // 2: dmid}
    for d in range(1, nz // 2):
        documents[-d], documents[d] = dr[d - 1], dl[d - 1]
    tables = {0: own_tab, -1: trp, 1: tlp, 2: tmid}

    def dots(distance, dx):
        docs, table = documents[distance], tables[dx]
        first = order.index(distance) * lrows
        at = (x + nx + dx) % nx * urows

        def body(i, _):
            line = first + at + i
            for q in range(0, LANES, 8):
                stage[pl.ds(q, 8), :] = jnp.concatenate(
                    [docs[pl.ds(srow[line, u] & (rows - 1), 1), :]
                     * table[pl.ds(sloc[line, u] & (table.shape[0] - 1), 1), :]
                     for u in range(q, q + 8)], 0)
            part[pl.ds(line, 1), :] = jnp.sum(stage[...].T, axis=0, keepdims=True)
            return 0

        lax.fori_loop(0, urows, body, 0)

    def part_copy(i):
        return copy(part.at[pl.ds(i * lrows, lrows)], s1buf.at[c], s1_s.at[i], s1_r.at[c], me, source[i])

    def hand_on(distance):
        i = order.index(distance)

        @pl.when(source[i] != c)
        def _():
            part_copy(i).start()

        @pl.when(source[i] == c)
        def _():
            s1buf[c] = part[pl.ds(i * lrows, lrows), :]

    def patch(k, before, after):
        patch_copy(k).wait_recv()
        new = pbuf[k - 1]
        rhs[0:SLOTS, 0:3 * LANES] = jnp.concatenate(split3(new[:SLOTS]), 1)
        chosen = new[SLOTS:SLOTS + 1]

        def body(i, _):
            after[cut(i), :] = patched(picked(i, chosen, 4 * LANES), before[cut(i), :])
            return 0

        lax.fori_loop(0, 7, body, 0)

    for d in (0, -1, 1):
        dots(d, 0)
    forward(zr, zl, 2, 0)
    xr[1, 1].wait_recv()
    xl[1, 0].wait_recv()
    patch(1, tr[0], trp)
    patch(3, tl[0], tlp)
    for d in (0, -1, 1):
        dots(d, -1)
        dots(d, 1)
    forward(zr, zl, 2, 1)
    for d in (-2, 2):
        for dx in (0, -1, 1):
            dots(d, dx)
    forward(zr, zl, 3, 0)
    xr[2, 0].wait_recv()
    xl[2, 1].wait_recv()
    patch(2, tmid, tmid)
    for d in (0, -1, 1, -2, 2):
        dots(d, 2)
        hand_on(d)
    forward(zr, zl, 3, 1)
    for d in (-3, 3):
        for dx in (0, -1, 1, 2):
            dots(d, dx)
        hand_on(d)
    zr[4, 0].wait_recv()
    zl[4, 1].wait_recv()
    for dx in (0, -1, 1, 2):
        dots(4, dx)
    hand_on(4)

    def part_wait(k, _):
        other = (c + k) % nc
        copy(full, s1buf.at[other], s1_s.at[0], s1_r.at[other], me, other).wait_recv()
        return 0

    lax.fori_loop(1, nc, part_wait, 0)
    total3 = s1buf[0]
    for k in range(1, nc):
        total3 = total3 + s1buf[k]
    full[...] = total3
    sums_at = lambda s: tbuf.at[pl.ds(pl.multiple_of(s * lrows, 8), lrows)]
    cross_start(full, sums_at, t_s, t_r)
    cross_wait(full, sums_at, t_s, t_r)

    table = jnp.concatenate(split3(tbuf[...]), 0)
    share = qrows // nc
    for g in range(share // 8):
        lows = [lo_ref[pl.ds(c * share + g * 8 + j, 1), :] for j in range(8)]
        tops = [hi_ref[pl.ds(c * share + g * 8 + j, 1), :] for j in range(8)]
        sel = jnp.concatenate(
            [(iota((LANES, LANES), 0).astype(F32) == v).astype(F32).astype(BF16) for v in lows], 1)
        got = jnp.dot(table, sel, preferred_element_type=F32)
        got = got[:qrows] + got[qrows:2 * qrows] + got[2 * qrows:]
        top_all = jnp.concatenate(tops, 1)
        line = jnp.sum(
            jnp.where(iota(got.shape, 0).astype(F32) == top_all, got, 0.0), axis=0, keepdims=True)
        factor = scale[pl.ds(c * (share // 8) + g, 1), :]
        for j in range(8):
            cos[j:j + 1, g * LANES:(g + 1) * LANES] = line[:, j * LANES:(j + 1) * LANES] * factor

    for ring_copies in (zr, zl, xr, xl):
        for one in ring_copies.values():
            one.wait_send()
    for k in range(1, nx):
        patch_copy(k).wait_send()
    for i in range(nz):
        @pl.when(source[i] != c)
        def _(i=i):
            part_copy(i).wait_send()


def on_device(nd, nc, embeddings, row_mask, block_cluster, candidates, old_centroids):
    rows, width = embeddings.shape
    owned = old_centroids.shape[0]
    nz = Z_CHIPS
    nx = nd // nz
    cands = candidates.shape[1]
    blocks = block_cluster.shape[0]
    qrows = rows * cands // LANES
    lrows = qrows // nz
    table_rows = 1 << (owned - 1).bit_length()
    vmem = lambda *s: pltpu.VMEM(s, F32)
    dma = lambda *s: pltpu.SemaphoreType.DMA(s)
    in_vmem = pl.BlockSpec(memory_space=pltpu.VMEM)
    scratch = [
        [vmem(rows, width)] * (nz // 2 - 1), [vmem(rows, width)] * (nz // 2 - 1), vmem(rows, width),
        [vmem(owned, width)], [vmem(owned, width)], *[vmem(table_rows, width)] * 4,
        vmem(blocks, LANES), vmem(nc, blocks, LANES), vmem(blocks, LANES),
        vmem(blocks, LANES), vmem(blocks, LANES),
        vmem(qrows, LANES), vmem(qrows, LANES), vmem(qrows, LANES), vmem(qrows, LANES), vmem(qrows, LANES),
        vmem(nd, 8, LANES), vmem(nd, 8, LANES), vmem(8, LANES), vmem(nc, 8, LANES),
        pltpu.VMEM((LANES, 7 * LANES), BF16), vmem(SLOTS + 8, LANES), vmem(nx - 1, SLOTS + 8, LANES),
        pltpu.VMEM((2, lrows, LANES), I32), pltpu.VMEM((nz, 2, lrows, LANES), I32),
        pltpu.SMEM((qrows, LANES), I32), pltpu.SMEM((qrows, LANES), I32),
        vmem(LANES, LANES), vmem(qrows, LANES), vmem(nc, lrows, LANES), vmem(lrows, LANES), vmem(qrows, LANES),
        dma(nz // 2, 2), dma(nz // 2, 2), dma(nz // 2, 2), dma(nz // 2, 2),
        dma(nx // 2, 2), dma(nx // 2, 2), dma(nx // 2, 2), dma(nx // 2, 2),
        dma(nc), dma(nc), dma(nc), dma(nc), dma(nd), dma(nd), dma(nx - 1), dma(nx - 1),
        dma(nc), dma(nz), dma(2, nz), dma(nz), dma(nc), dma(nc), dma(nz),
    ]
    sums, counts, cents, cosines = pl.pallas_call(
        functools.partial(kernel, nd, nz, nc),
        out_shape=(
            jax.ShapeDtypeStruct((owned, width), F32),
            jax.ShapeDtypeStruct((-(-owned // (8 * LANES)) * 8, LANES), I32),
            jax.ShapeDtypeStruct((owned, width), F32),
            jax.ShapeDtypeStruct((cands, rows // nc), F32),
        ),
        in_specs=[in_vmem] * 4 + [pl.BlockSpec(memory_space=pltpu.SMEM)],
        out_specs=(in_vmem,) * 4,
        scratch_shapes=scratch,
        compiler_params=pltpu.CompilerParams(
            collective_id=0, has_side_effects=True, vmem_limit_bytes=52 << 20),
        name="update",
    )(embeddings, old_centroids, row_mask.reshape(blocks, rows // blocks), candidates.T, block_cluster)
    return sums, counts.reshape(-1)[:owned], cents, cosines.T


def solution(mesh):
    placed = (P("doc", "cent"), P("doc"), P("doc"), P("doc", None), P("doc", "cent"))
    return jax.shard_map(
        functools.partial(on_device, mesh.shape["doc"], mesh.shape["cent"]),
        mesh=mesh,
        in_specs=placed,
        out_specs=(P("doc", "cent"), P("doc"), P("doc", "cent"), P(("doc", "cent"), None)),
        check_vma=False,
    )
```

```python
import functools

import jax
import jax.numpy as jnp
from jax import lax
from jax.experimental import pallas as pl
from jax.experimental.pallas import tpu as pltpu
from jax.sharding import PartitionSpec as P

MESH = pl.DeviceIdType.MESH
F32, BF16, I32 = jnp.float32, jnp.bfloat16, jnp.int32
Z_CHIPS = 8
LANES = 128
SLOTS = 64
NT = (((1,), (1,)), ((), ()))


def iota(shape, dim):
    return lax.broadcasted_iota(I32, shape, dim)


def split2(v):
    a = v.astype(BF16)
    return a, (v - a.astype(F32)).astype(BF16)


def split3(v):
    a = v.astype(BF16)
    rest = v - a.astype(F32)
    b = rest.astype(BF16)
    return a, b, (rest - b.astype(F32)).astype(BF16)


def rhs_of(values):
    return jnp.concatenate([values, jnp.ones((2 * LANES, LANES), BF16)], 1)


def one_hot(chosen, first, step):
    hit = (iota((step, LANES), 0) + first).astype(F32) == chosen
    return hit.astype(F32).astype(BF16)


def replaced(chosen, rhs, first, before):
    hit = one_hot(chosen, first, before.shape[0])
    out = jnp.dot(jnp.concatenate([hit, hit], 1), rhs, preferred_element_type=F32)
    return jnp.where(out[:, LANES:] > 0, out[:, :LANES], before)


def expand(slots, old, ms, cnt, cen):
    step = ms.shape[0]
    i = pl.program_id(0)
    empty = jnp.zeros((LANES - SLOTS, LANES), BF16)
    parts = [split2(slots[k * SLOTS:(k + 1) * SLOTS, :]) for k in (0, 1)]
    rhs = jnp.concatenate([jnp.concatenate([p[k] if j == 0 else empty for k in (0, 1) for j in (0, 1)], 0)
                           for p in parts], 1)
    chosen = slots[2 * SLOTS:2 * SLOTS + 1, :]
    hit = one_hot(chosen, i * step, step)
    twice = jnp.concatenate([hit, hit], 1)
    out = jnp.dot(twice, jnp.concatenate([rhs, jnp.ones((2 * LANES, LANES), BF16)], 1),
                  preferred_element_type=F32)
    ms[...] = out[:, :LANES]
    cen[...] = jnp.where(out[:, 2 * LANES:] > 0, out[:, LANES:2 * LANES], old[...])

    @pl.when(i == 0)
    def _():
        ids = slots[2 * SLOTS + 8:2 * SLOTS + 9, :]
        ids_top = jnp.floor(ids * (1.0 / LANES))
        count_left = jnp.where(iota(cnt.shape, 0).astype(F32) == ids_top,
                               slots[2 * SLOTS + 16:2 * SLOTS + 17, :], 0.0).astype(BF16)
        count_right = (iota((LANES, LANES), 0).astype(F32) == ids - ids_top * LANES).astype(F32).astype(BF16)
        cnt[...] = lax.dot_general(count_left, count_right, NT, preferred_element_type=F32).astype(I32)


def kernel(
    nd, nz, nc,
    emb_in, old_in, live_hbm, cand_hbm, blk_hbm,
    found_slots, cos,
    emb, old, live_in, cand, blk,
    dr, dl, dmid, tr, tl, own_tab, tmid, trp, tlp,
    sq_src, sq_buf, scale, bsum, bcnt, pos, loc_hi, loc_lo, hi_ref, lo_ref,
    msgs, rbuf, sq2_src, sq2_buf, rhs, psend, pbuf, lsend, lbuf, srow, sloc,
    stage, part, s1buf, full, tbuf, sel,
    zr_s, zr_r, zl_s, zl_r, xr_s, xr_r, xl_s, xl_r,
    sq_s, sq_r, sq2_s, sq2_r, a2a_s, a2a_r, p_s, p_r, l_s, l_r, sm_sem, s1_s, s1_r, t_s, t_r, in_sem,
):
    nx = nd // nz
    rows, owned = emb_in.shape[0], old_in.shape[0]
    blocks = blk.shape[0]
    me = lax.axis_index("doc")
    c = lax.axis_index("cent")
    x, z = me // nz, me % nz
    per_z = pos.shape[0] * LANES // nz
    lrows = per_z // LANES
    per_owner = per_z // nx
    urows = lrows // nx

    def copy(src, dst, ssem, rsem, doc, cent):
        return pltpu.make_async_remote_copy(
            src_ref=src, dst_ref=dst, send_sem=ssem, recv_sem=rsem,
            device_id=(doc, cent), device_id_type=MESH,
        )

    loads = [pltpu.make_async_copy(a, b, in_sem.at[i]) for i, (a, b) in enumerate(
        ((emb_in, emb), (cand_hbm, cand), (live_hbm, live_in), (blk_hbm, blk), (old_in, old)))]
    for load in loads:
        load.start()

    bar = pltpu.get_barrier_semaphore()

    def greet(doc, cent):
        pl.semaphore_signal(bar, inc=1, device_id=(doc, cent), device_id_type=MESH)

    lax.fori_loop(1, nd, lambda k, _: (greet((me + k) % nd, c), 0)[1], 0)
    lax.fori_loop(1, nc, lambda k, _: (greet(me, (c + k) % nc), 0)[1], 0)

    @pl.when(c != z)
    def _():
        lax.fori_loop(1, nz, lambda k, _: (greet(x * nz + (z + k) % nz, z), 0)[1], 0)
        pl.semaphore_wait(bar, nd - 1 + nc - 1 + nz - 1)

    @pl.when(c == z)
    def _():
        pl.semaphore_wait(bar, nd - 1 + nc - 1)

    def ring(n, own, right, left, mid, rs, rr, ls, lr, right_id, left_id):
        half = own.shape[0] // 2
        last = n // 2
        out_r, out_l = {}, {}
        for s in range(1, last + 1):
            src_r = own if s == 1 else right[s - 2]
            src_l = own if s == 1 else left[s - 2]
            for h in (0, 1):
                cut = pl.ds(h * half, half)
                if s < last or h == 0:
                    dst = (right[s - 1] if s < last else mid).at[cut]
                    out_r[s, h] = copy(src_r.at[cut], dst, rs.at[s - 1, h], rr.at[s - 1, h], right_id, c)
                if s < last or h == 1:
                    dst = (left[s - 1] if s < last else mid).at[cut]
                    out_l[s, h] = copy(src_l.at[cut], dst, ls.at[s - 1, h], lr.at[s - 1, h], left_id, c)
        return out_r, out_l

    zr, zl = ring(nz, emb_in, dr, dl, dmid, zr_s, zr_r, zl_s, zl_r,
                  x * nz + (z + 1) % nz, x * nz + (z + nz - 1) % nz)
    xr, xl = ring(nx, old_in, tr, tl, tmid, xr_s, xr_r, xl_s, xl_r,
                  (x + 1) % nx * nz + z, (x + nx - 1) % nx * nz + z)

    def forward(right, left, s, h):
        right[s, h].wait_recv()
        if (s + 1, h) in right:
            right[s + 1, h].start()
        left[s, 1 - h].wait_recv()
        if (s + 1, 1 - h) in left:
            left[s + 1, 1 - h].start()

    zr[1, 0].start()
    zl[1, 1].start()
    xr[1, 0].start()
    xl[1, 1].start()

    def cent_copy(src, buf, ss, rs, k):
        return copy(src, buf.at[c], ss.at[k], rs.at[c], me, (c + k) % nc)

    def cent_start(src, buf, ss, rs):
        lax.fori_loop(1, nc, lambda k, _: (cent_copy(src, buf, ss, rs, k).start(), 0)[1], 0)
        buf[c] = src[...]

    def cent_wait(src, buf, ss, rs):
        def body(k, _):
            other = (c + k) % nc
            copy(src, buf.at[other], ss.at[k], rs.at[other], me, other).wait()
            return 0
        lax.fori_loop(1, nc, body, 0)

    def cross_copy(src, dst, ss, rs, k):
        return copy(src, dst(z), ss.at[k], rs.at[z], x * nz + c, (c + k) % nc)

    def cross_start(src, dst, ss, rs):
        lax.fori_loop(1, nc, lambda k, _: (cross_copy(src, dst, ss, rs, k).start(), 0)[1], 0)

        @pl.when(c != z)
        def _():
            cross_copy(src, dst, ss, rs, 0).start()

        @pl.when(c == z)
        def _():
            dst(z)[...] = src[...]

    def cross_wait(src, dst, ss, rs):
        def body(k, _):
            other = (z + k) % nz
            copy(src, dst(other), ss.at[k], rs.at[other], x * nz + c, (c + k) % nc).wait()
            return 0
        lax.fori_loop(1, nz, body, 0)

        @pl.when(c != z)
        def _():
            cross_copy(src, dst, ss, rs, 0).wait()

    for table in (own_tab, tmid, trp, tlp):
        table[owned:, :] = jnp.zeros((table.shape[0] - owned, LANES), F32)

    for load in loads[:4]:
        load.wait()
    for b in range(blocks):
        t = emb[b * LANES:(b + 1) * LANES, :].T
        sq_src[b:b + 1, :] = jnp.sum(t * t, axis=0, keepdims=True)
    cent_start(sq_src, sq_buf, sq_s, sq_r)
    zr[1, 1].start()
    zl[1, 0].start()
    xr[1, 1].start()
    xl[1, 0].start()

    ids = jnp.concatenate([cand[:, LANES * i:LANES * (i + 1)] for i in range(rows // LANES)], 0).astype(F32)
    qrows = ids.shape[0]
    owner = jnp.floor((ids + 0.5) * (1.0 / owned))
    loc = ids - owner * owned
    loc_top = jnp.floor(loc * (1.0 / LANES))
    loc_hi[...] = loc_top
    loc_lo[...] = loc - loc_top * LANES
    upper_ones = jnp.concatenate(
        [(iota((LANES, LANES), 0) < iota((LANES, LANES), 1)).astype(F32), jnp.ones((LANES, LANES), F32)],
        0).astype(BF16)
    lower = (iota((qrows, qrows), 0) > iota((qrows, qrows), 1)).astype(F32).astype(BF16)
    places = jnp.zeros((qrows, LANES), F32)
    for first in range(0, nd, 8):
        masks = [(owner == float(m)).astype(F32) for m in range(first, first + 8)]
        coded = [v.astype(BF16) for v in masks]
        above = jnp.dot(lower, jnp.concatenate(coded, 1), preferred_element_type=F32).astype(BF16)
        both = jnp.concatenate(
            [jnp.concatenate([coded[m], above[:, m * LANES:(m + 1) * LANES]], 1) for m in range(8)], 0)
        rank = jnp.dot(both, upper_ones, preferred_element_type=F32)
        for m in range(8):
            start = float((first + m) % nz * per_z + (first + m) // nz * per_owner)
            places = places + masks[m] * (rank[m * qrows:(m + 1) * qrows] + start)
    pos[...] = places
    top = jnp.floor(pos[...] * (1.0 / LANES))
    hi_ref[...] = top
    lo_ref[...] = pos[...] - top * LANES

    cent_wait(sq_src, sq_buf, sq_s, sq_r)
    total = sq_buf[0]
    for k in range(1, nc):
        total = total + sq_buf[k]
    alive = live_in[...].astype(F32)
    scale[...] = lax.rsqrt(total + 1e-6) * alive

    weights = jnp.concatenate([scale[...], jnp.zeros((LANES - blocks, LANES), F32)], 0).T
    for b in range(blocks):
        bsum[b:b + 1, :] = jnp.sum(
            weights[:, b:b + 1] * emb[b * LANES:(b + 1) * LANES, :], axis=0, keepdims=True)
    bcnt[...] = jnp.broadcast_to(jnp.sum(alive, axis=1, keepdims=True), (blocks, LANES))
    owners = [blk[b] // owned for b in range(blocks)]
    place_of = [jnp.int32(0)] + [
        jnp.where(owners[b] == owners[b - 1], 1, 0) for b in range(1, blocks)]
    local = [(blk[b] - owners[b] * owned).astype(F32) for b in range(blocks)]

    def message(i, _):
        line = iota((8, LANES), 0)
        tiles = [jnp.zeros((8, LANES), F32)] * 4
        for b in range(blocks):
            content = jnp.where(line < 2, bsum[b:b + 1, :], jnp.where(line < 4, local[b], bcnt[b:b + 1, :]))
            for k in range(4):
                at = jnp.where(owners[b] == i * 4 + k, place_of[b], 8)
                mine = (line == at) | (line == at + 2) | (line == at + 4)
                tiles[k] = jnp.where(mine, content, tiles[k])
        for k in range(4):
            msgs[i * 4 + k] = tiles[k]
        return 0

    lax.fori_loop(0, nd // 4, message, 0)

    def a2a_start(k, _):
        to = (me + k) % nd
        copy(msgs.at[to], rbuf.at[me], a2a_s.at[k], a2a_r.at[me], to, c).start()
        return 0

    def a2a_wait(k, _):
        other = (me + k) % nd
        copy(msgs.at[other], rbuf.at[other], a2a_s.at[k], a2a_r.at[other], other, c).wait()
        return 0

    lax.fori_loop(1, nd, a2a_start, 0)
    rbuf[me] = msgs[me]

    shift = (c * lrows).astype(F32)
    lane_row = iota((1, LANES), 1).astype(F32)

    def lists(i, acc):
        left_parts, right_parts = [], []
        for j in range(32):
            q = pl.ds(i * 32 + j, 1)
            at = (iota((lrows, LANES), 0).astype(F32) == hi_ref[q, :] - shift).astype(F32)
            left_parts.append(jnp.concatenate(
                [at * (i * 4 + j // 8).astype(F32), at * lane_row, at * loc_hi[q, :], at * loc_lo[q, :]], 0).astype(BF16))
            right_parts.append(
                (iota((LANES, LANES), 0).astype(F32) == lo_ref[q, :]).astype(F32).astype(BF16))
        return acc + lax.dot_general(
            jnp.concatenate(left_parts, 1), jnp.concatenate(right_parts, 1), NT, preferred_element_type=F32)

    found = lax.fori_loop(0, qrows // 32, lists, jnp.zeros((4 * lrows, LANES), F32))
    lsend[0] = (found[:lrows] * LANES + found[lrows:2 * lrows]).astype(I32)
    lsend[1] = (found[2 * lrows:3 * lrows] * LANES + found[3 * lrows:]).astype(I32)
    lists_at = lambda s: lbuf.at[s]
    cross_start(lsend, lists_at, l_s, l_r)

    forward(zr, zl, 1, 0)
    forward(xr, xl, 1, 0)
    forward(zr, zl, 1, 1)
    lax.fori_loop(1, nd, a2a_wait, 0)

    def slots(first, empty):
        return jnp.concatenate(
            [rbuf[:, first, :], rbuf[:, first + 1, :],
             jnp.full((LANES - 2 * nd, LANES), empty, F32)], 0)

    sums, slot_ids, slot_counts = slots(0, 0.0), slots(2, -1.0), slots(4, 0.0)
    slot_ids = jnp.where(slot_counts > 0, slot_ids, -1.0)
    ids_lane = slot_ids.T
    same = jnp.where((slot_ids == ids_lane) & (slot_counts > 0), 1.0, 0.0)
    group = jnp.dot(same.astype(BF16), jnp.concatenate(split3(sums), 1), preferred_element_type=F32)
    group = group[:, :LANES] + group[:, LANES:2 * LANES] + group[:, 2 * LANES:]
    square = group * group
    sq2_src[...] = jnp.broadcast_to(jnp.sum(square.T, axis=0, keepdims=True), (8, LANES))
    cent_start(sq2_src, sq2_buf, sq2_s, sq2_r)

    earlier = jnp.sum(
        jnp.where(iota((LANES, LANES), 0) < iota((LANES, LANES), 1), same, 0.0), axis=0, keepdims=True)
    first_ids = jnp.where(earlier > 0, -1.0, ids_lane[0:1])
    counts_lane = slot_counts.T[0:1]
    cent_wait(sq2_src, sq2_buf, sq2_s, sq2_r)
    total2 = sq2_buf[0]
    for k in range(1, nc):
        total2 = total2 + sq2_buf[k]
    inverse = lax.rsqrt(jnp.broadcast_to(total2[0:1], (LANES, LANES)) + 1e-6).T
    normal = group * inverse
    psend[0:SLOTS, :] = normal[:SLOTS]
    psend[SLOTS:SLOTS + 8, :] = jnp.broadcast_to(first_ids, (8, LANES))

    def patch_copy(k):
        return copy(psend, pbuf.at[k - 1], p_s.at[k - 1], p_r.at[k - 1], (x + k) % nx * nz + z, c)

    for k in range(1, nx):
        patch_copy(k).start()

    found_slots[0:SLOTS, :] = group[:SLOTS]
    found_slots[SLOTS:2 * SLOTS, :] = normal[:SLOTS]
    found_slots[2 * SLOTS:2 * SLOTS + 8, :] = jnp.broadcast_to(first_ids, (8, LANES))
    found_slots[2 * SLOTS + 8:2 * SLOTS + 16, :] = jnp.broadcast_to(ids_lane[0:1], (8, LANES))
    found_slots[2 * SLOTS + 16:2 * SLOTS + 24, :] = slot_counts.T[0:8]

    step = owned // 7
    rhs[...] = rhs_of(jnp.zeros((2 * LANES, LANES), BF16))

    def patch_rows(new, chosen, before, after):
        high, low = split2(new)
        rhs[0:SLOTS, 0:LANES] = high
        rhs[LANES:LANES + SLOTS, 0:LANES] = low

        def body(i, _):
            at = pl.ds(pl.multiple_of(i * step, 8), step)
            after[at, :] = replaced(chosen, rhs[...], i * step, before[at, :])
            return 0

        lax.fori_loop(0, 7, body, 0)

    loads[4].wait()
    patch_rows(normal[:SLOTS], first_ids, old, own_tab)

    cross_wait(lsend, lists_at, l_s, l_r)
    order = [0] + [d * s for d in range(1, nz // 2) for s in (-1, 1)] + [nz // 2]
    source = [(z + nz + d) % nz for d in order]
    for i in range(nz):
        here = pl.ds(i * lrows, lrows)
        pltpu.make_async_copy(lbuf.at[source[i], 0], srow.at[here], sm_sem.at[0, i]).start()
        pltpu.make_async_copy(lbuf.at[source[i], 1], sloc.at[here], sm_sem.at[1, i]).start()
    for i in range(nz):
        here = pl.ds(i * lrows, lrows)
        pltpu.make_async_copy(lbuf.at[source[i], 0], srow.at[here], sm_sem.at[0, i]).wait()
        pltpu.make_async_copy(lbuf.at[source[i], 1], sloc.at[here], sm_sem.at[1, i]).wait()

    documents = {0: emb, nz // 2: dmid}
    for d in range(1, nz // 2):
        documents[-d], documents[d] = dr[d - 1], dl[d - 1]
    tables = {0: own_tab, -1: trp, 1: tlp, 2: tmid}

    def dots(distance, dx):
        docs, table = documents[distance], tables[dx]
        first = order.index(distance) * lrows
        at = (x + nx + dx) % nx * urows

        def body(i, _):
            line = first + at + i
            for q in range(0, LANES, 8):
                stage[pl.ds(q, 8), :] = jnp.concatenate(
                    [docs[pl.ds(srow[line, u] & (rows - 1), 1), :]
                     * table[pl.ds(sloc[line, u] & (table.shape[0] - 1), 1), :]
                     for u in range(q, q + 8)], 0)
            part[pl.ds(line, 1), :] = jnp.sum(stage[...].T, axis=0, keepdims=True)
            return 0

        lax.fori_loop(0, urows, body, 0)

    def part_copy(i):
        return copy(part.at[pl.ds(i * lrows, lrows)], s1buf.at[c], s1_s.at[i], s1_r.at[c], me, source[i])

    def hand_on(distance):
        i = order.index(distance)

        @pl.when(source[i] != c)
        def _():
            part_copy(i).start()

        @pl.when(source[i] == c)
        def _():
            s1buf[c] = part[pl.ds(i * lrows, lrows), :]

    def patch(k, before, after):
        patch_copy(k).wait_recv()
        new = pbuf[k - 1]
        patch_rows(new[:SLOTS], new[SLOTS:SLOTS + 1], before, after)

    for d in (0, -1, 1):
        dots(d, 0)
    forward(zr, zl, 2, 0)
    xr[1, 1].wait_recv()
    xl[1, 0].wait_recv()
    patch(1, tr[0], trp)
    patch(3, tl[0], tlp)
    for d in (0, -1, 1):
        dots(d, -1)
        dots(d, 1)
    forward(zr, zl, 2, 1)
    for d in (-2, 2):
        for dx in (0, -1, 1):
            dots(d, dx)
    forward(zr, zl, 3, 0)
    xr[2, 0].wait_recv()
    xl[2, 1].wait_recv()
    patch(2, tmid, tmid)
    for d in (0, -1, 1, -2, 2):
        dots(d, 2)
        hand_on(d)
    forward(zr, zl, 3, 1)
    for d in (-3, 3):
        for dx in (0, -1, 1, 2):
            dots(d, dx)
        hand_on(d)
    share = qrows // nc
    tops = []
    for g in range(share // 8):
        own = [pl.ds(c * share + g * 8 + j, 1) for j in range(8)]
        sel[:, g * 8 * LANES:(g + 1) * 8 * LANES] = jnp.concatenate(
            [(iota((LANES, LANES), 0).astype(F32) == lo_ref[v, :]).astype(F32).astype(BF16) for v in own], 1)
        tops.append(jnp.concatenate([hi_ref[v, :] for v in own], 1))
    zr[4, 0].wait_recv()
    zl[4, 1].wait_recv()
    for dx in (0, -1, 1, 2):
        dots(4, dx)
    hand_on(4)

    def part_wait(k, _):
        other = (c + k) % nc
        copy(full, s1buf.at[other], s1_s.at[0], s1_r.at[other], me, other).wait_recv()
        return 0

    lax.fori_loop(1, nc, part_wait, 0)
    total3 = s1buf[0]
    for k in range(1, nc):
        total3 = total3 + s1buf[k]
    full[...] = total3
    sums_at = lambda s: tbuf.at[pl.ds(pl.multiple_of(s * lrows, 8), lrows)]
    cross_start(full, sums_at, t_s, t_r)
    cross_wait(full, sums_at, t_s, t_r)

    table = jnp.concatenate(split2(tbuf[...]), 0)
    for g in range(share // 8):
        got = jnp.dot(table, sel[:, g * 8 * LANES:(g + 1) * 8 * LANES], preferred_element_type=F32)
        got = got[:qrows] + got[qrows:]
        line = jnp.sum(
            jnp.where(iota(got.shape, 0).astype(F32) == tops[g], got, 0.0), axis=0, keepdims=True)
        factor = scale[pl.ds(c * (share // 8) + g, 1), :]
        for j in range(8):
            cos[j:j + 1, g * LANES:(g + 1) * LANES] = line[:, j * LANES:(j + 1) * LANES] * factor

    for ring_copies in (zr, zl, xr, xl):
        for one in ring_copies.values():
            one.wait_send()
    for k in range(1, nx):
        patch_copy(k).wait_send()
    for i in range(nz):
        @pl.when(source[i] != c)
        def _(i=i):
            part_copy(i).wait_send()


def on_device(nd, nc, embeddings, row_mask, block_cluster, candidates, old_centroids):
    rows, width = embeddings.shape
    owned = old_centroids.shape[0]
    nz = Z_CHIPS
    nx = nd // nz
    cands = candidates.shape[1]
    blocks = block_cluster.shape[0]
    qrows = rows * cands // LANES
    lrows = qrows // nz
    table_rows = 1 << (owned - 1).bit_length()
    vmem = lambda *s: pltpu.VMEM(s, F32)
    dma = lambda *s: pltpu.SemaphoreType.DMA(s)
    in_vmem = pl.BlockSpec(memory_space=pltpu.VMEM)
    scratch = [
        vmem(rows, width), vmem(owned, width), pltpu.VMEM((blocks, LANES), I32), pltpu.VMEM((cands, rows), I32),
        pltpu.SMEM((blocks,), I32),
        [vmem(rows, width)] * (nz // 2 - 1), [vmem(rows, width)] * (nz // 2 - 1), vmem(rows, width),
        [vmem(owned, width)], [vmem(owned, width)], *[vmem(table_rows, width)] * 4,
        vmem(blocks, LANES), vmem(nc, blocks, LANES), vmem(blocks, LANES),
        vmem(blocks, LANES), vmem(blocks, LANES),
        vmem(qrows, LANES), vmem(qrows, LANES), vmem(qrows, LANES), vmem(qrows, LANES), vmem(qrows, LANES),
        vmem(nd, 8, LANES), vmem(nd, 8, LANES), vmem(8, LANES), vmem(nc, 8, LANES),
        pltpu.VMEM((2 * LANES, 2 * LANES), BF16), vmem(SLOTS + 8, LANES), vmem(nx - 1, SLOTS + 8, LANES),
        pltpu.VMEM((2, lrows, LANES), I32), pltpu.VMEM((nz, 2, lrows, LANES), I32),
        pltpu.SMEM((qrows, LANES), I32), pltpu.SMEM((qrows, LANES), I32),
        vmem(LANES, LANES), vmem(qrows, LANES), vmem(nc, lrows, LANES), vmem(lrows, LANES), vmem(qrows, LANES),
        pltpu.VMEM((LANES, rows * cands // nc), BF16),
        dma(nz // 2, 2), dma(nz // 2, 2), dma(nz // 2, 2), dma(nz // 2, 2),
        dma(nx // 2, 2), dma(nx // 2, 2), dma(nx // 2, 2), dma(nx // 2, 2),
        dma(nc), dma(nc), dma(nc), dma(nc), dma(nd), dma(nd), dma(nx - 1), dma(nx - 1),
        dma(nc), dma(nz), dma(2, nz), dma(nz), dma(nc), dma(nc), dma(nz), dma(5),
    ]
    slots, cosines = pl.pallas_call(
        functools.partial(kernel, nd, nz, nc),
        out_shape=(
            jax.ShapeDtypeStruct((2 * SLOTS + 24, width), F32),
            jax.ShapeDtypeStruct((cands, rows // nc), F32),
        ),
        in_specs=[pl.BlockSpec(memory_space=pltpu.HBM)] * 5,
        out_specs=(in_vmem,) * 2,
        scratch_shapes=scratch,
        compiler_params=pltpu.CompilerParams(
            collective_id=0, has_side_effects=True, vmem_limit_bytes=65536 * 1000),
        name="update",
    )(embeddings, old_centroids, row_mask.reshape(blocks, rows // blocks), candidates.T, block_cluster)
    steps = 4
    step = owned // steps
    table_block = pl.BlockSpec((step, width), lambda i: (i, 0))
    whole = lambda shape: pl.BlockSpec(shape, lambda i: (0, 0))
    counts_shape = (-(-owned // (8 * LANES)) * 8, LANES)
    sums, counts, cents = pl.pallas_call(
        expand,
        grid=(steps,),
        out_shape=(
            jax.ShapeDtypeStruct((owned, width), F32),
            jax.ShapeDtypeStruct(counts_shape, I32),
            jax.ShapeDtypeStruct((owned, width), F32),
        ),
        in_specs=[whole(slots.shape), table_block],
        out_specs=(table_block, whole(counts_shape), table_block),
        compiler_params=pltpu.CompilerParams(vmem_limit_bytes=16 << 20),
        name="expand",
    )(slots, old_centroids)
    return sums, counts.reshape(-1)[:owned], cents, cosines.T


def solution(mesh):
    placed = (P("doc", "cent"), P("doc"), P("doc"), P("doc", None), P("doc", "cent"))
    return jax.shard_map(
        functools.partial(on_device, mesh.shape["doc"], mesh.shape["cent"]),
        mesh=mesh,
        in_specs=placed,
        out_specs=(P("doc", "cent"), P("doc"), P("doc", "cent"), P(("doc", "cent"), None)),
        check_vma=False,
    )
```

```python
import functools

import jax
import jax.numpy as jnp
from jax import lax
from jax.experimental import pallas as pl
from jax.experimental.pallas import tpu as pltpu
from jax.sharding import PartitionSpec as P

MESH = pl.DeviceIdType.MESH
F32, BF16, I32 = jnp.float32, jnp.bfloat16, jnp.int32
Z_CHIPS = 8
LANES = 128
SLOTS = 64
NT = (((1,), (1,)), ((), ()))


def iota(shape, dim):
    return lax.broadcasted_iota(I32, shape, dim)


def split2(v):
    a = v.astype(BF16)
    return a, (v - a.astype(F32)).astype(BF16)


def split3(v):
    a = v.astype(BF16)
    rest = v - a.astype(F32)
    b = rest.astype(BF16)
    return a, b, (rest - b.astype(F32)).astype(BF16)


def rhs_of(values):
    return jnp.concatenate([values, jnp.ones((2 * LANES, LANES), BF16)], 1)


def one_hot(chosen, first, step):
    hit = (iota((step, LANES), 0) + first).astype(F32) == chosen
    return hit.astype(F32).astype(BF16)


def replaced(chosen, rhs, first, before):
    hit = one_hot(chosen, first, before.shape[0])
    out = jnp.dot(jnp.concatenate([hit, hit], 1), rhs, preferred_element_type=F32)
    return jnp.where(out[:, LANES:] > 0, out[:, :LANES], before)


def expand(slots, old, ms, cnt, cen):
    step = ms.shape[0]
    i = pl.program_id(0)
    empty = jnp.zeros((LANES - SLOTS, LANES), BF16)
    parts = [split2(slots[k * SLOTS:(k + 1) * SLOTS, :]) for k in (0, 1)]
    rhs = jnp.concatenate([jnp.concatenate([p[k] if j == 0 else empty for k in (0, 1) for j in (0, 1)], 0)
                           for p in parts], 1)
    chosen = slots[2 * SLOTS:2 * SLOTS + 1, :]
    hit = one_hot(chosen, i * step, step)
    twice = jnp.concatenate([hit, hit], 1)
    out = jnp.dot(twice, jnp.concatenate([rhs, jnp.ones((2 * LANES, LANES), BF16)], 1),
                  preferred_element_type=F32)
    ms[...] = out[:, :LANES]
    cen[...] = jnp.where(out[:, 2 * LANES:] > 0, out[:, LANES:2 * LANES], old[...])

    @pl.when(i == 0)
    def _():
        ids = slots[2 * SLOTS + 8:2 * SLOTS + 9, :]
        ids_top = jnp.floor(ids * (1.0 / LANES))
        count_left = jnp.where(iota(cnt.shape, 0).astype(F32) == ids_top,
                               slots[2 * SLOTS + 16:2 * SLOTS + 17, :], 0.0).astype(BF16)
        count_right = (iota((LANES, LANES), 0).astype(F32) == ids - ids_top * LANES).astype(F32).astype(BF16)
        cnt[...] = lax.dot_general(count_left, count_right, NT, preferred_element_type=F32).astype(I32)


def kernel(
    nd, nz, nc,
    emb_in, old_in, live_hbm, cand_hbm, blk_hbm,
    found_slots, cos,
    emb, old, live_in, cand, blk,
    dr, dl, dmid, tr, tl, own_tab, tmid, trp, tlp,
    sq_src, sq_buf, scale, bsum, bcnt, pos, loc_hi, loc_lo, hi_ref, lo_ref,
    msgs, rbuf, sq2_src, sq2_buf, rhs, psend, pbuf, lsend, lbuf, srow, sloc,
    stage, part, s1buf, full, tbuf, sel, obuf,
    zr_s, zr_r, zl_s, zl_r, xr_s, xr_r, xl_s, xl_r,
    sq_s, sq_r, sq2_s, sq2_r, a2a_s, a2a_r, p_s, p_r, l_s, l_r, sm_sem, s1_s, s1_r, t_s, t_r, in_sem, o_s, o_r,
):
    nx = nd // nz
    rows, owned = emb_in.shape[0], old_in.shape[0]
    blocks = blk.shape[0]
    me = lax.axis_index("doc")
    c = lax.axis_index("cent")
    x, z = me // nz, me % nz
    per_z = pos.shape[0] * LANES // nz
    lrows = per_z // LANES
    per_owner = per_z // nx
    urows = lrows // nx

    def copy(src, dst, ssem, rsem, doc, cent):
        return pltpu.make_async_remote_copy(
            src_ref=src, dst_ref=dst, send_sem=ssem, recv_sem=rsem,
            device_id=(doc, cent), device_id_type=MESH,
        )

    loads = [pltpu.make_async_copy(a, b, in_sem.at[i]) for i, (a, b) in enumerate(
        ((emb_in, emb), (cand_hbm, cand), (live_hbm, live_in), (blk_hbm, blk), (old_in, old)))]
    for load in loads:
        load.start()

    bar = pltpu.get_barrier_semaphore()

    def greet(doc, cent):
        pl.semaphore_signal(bar, inc=1, device_id=(doc, cent), device_id_type=MESH)

    lax.fori_loop(1, nd, lambda k, _: (greet((me + k) % nd, c), 0)[1], 0)
    lax.fori_loop(1, nc, lambda k, _: (greet(me, (c + k) % nc), 0)[1], 0)

    facing = (z + nz // 2) % nz
    lax.fori_loop(1, nc, lambda k, _: (greet(x * nz + facing, (c + k) % nc), 0)[1], 0)

    @pl.when(c != z)
    def _():
        lax.fori_loop(1, nz, lambda k, _: (greet(x * nz + (z + k) % nz, z), 0)[1], 0)
        pl.semaphore_wait(bar, nd - 1 + 2 * (nc - 1) + nz - 1)

    @pl.when(c == z)
    def _():
        pl.semaphore_wait(bar, nd - 1 + 2 * (nc - 1))

    def ring(n, own, right, left, mid, rs, rr, ls, lr, right_id, left_id):
        half = own.shape[0] // 2
        last = n // 2
        out_r, out_l = {}, {}
        for s in range(1, last + 1):
            src_r = own if s == 1 else right[s - 2]
            src_l = own if s == 1 else left[s - 2]
            for h in (0, 1):
                cut = pl.ds(h * half, half)
                if s < last or h == 0:
                    dst = (right[s - 1] if s < last else mid).at[cut]
                    out_r[s, h] = copy(src_r.at[cut], dst, rs.at[s - 1, h], rr.at[s - 1, h], right_id, c)
                if s < last or h == 1:
                    dst = (left[s - 1] if s < last else mid).at[cut]
                    out_l[s, h] = copy(src_l.at[cut], dst, ls.at[s - 1, h], lr.at[s - 1, h], left_id, c)
        return out_r, out_l

    zr, zl = ring(nz, emb_in, dr, dl, dmid, zr_s, zr_r, zl_s, zl_r,
                  x * nz + (z + 1) % nz, x * nz + (z + nz - 1) % nz)
    xr, xl = ring(nx, old_in, tr, tl, tmid, xr_s, xr_r, xl_s, xl_r,
                  (x + 1) % nx * nz + z, (x + nx - 1) % nx * nz + z)

    def forward(right, left, s, h):
        right[s, h].wait_recv()
        if (s + 1, h) in right:
            right[s + 1, h].start()
        left[s, 1 - h].wait_recv()
        if (s + 1, 1 - h) in left:
            left[s + 1, 1 - h].start()

    zr[1, 0].start()
    zl[1, 1].start()
    xr[1, 0].start()
    xl[1, 1].start()

    def cent_copy(src, buf, ss, rs, k):
        return copy(src, buf.at[c], ss.at[k], rs.at[c], me, (c + k) % nc)

    def cent_start(src, buf, ss, rs):
        lax.fori_loop(1, nc, lambda k, _: (cent_copy(src, buf, ss, rs, k).start(), 0)[1], 0)
        buf[c] = src[...]

    def cent_wait(src, buf, ss, rs):
        def body(k, _):
            other = (c + k) % nc
            copy(src, buf.at[other], ss.at[k], rs.at[other], me, other).wait()
            return 0
        lax.fori_loop(1, nc, body, 0)

    def cross_copy(src, dst, ss, rs, k):
        return copy(src, dst(z), ss.at[k], rs.at[z], x * nz + c, (c + k) % nc)

    def cross_start(src, dst, ss, rs):
        lax.fori_loop(1, nc, lambda k, _: (cross_copy(src, dst, ss, rs, k).start(), 0)[1], 0)

        @pl.when(c != z)
        def _():
            cross_copy(src, dst, ss, rs, 0).start()

        @pl.when(c == z)
        def _():
            dst(z)[...] = src[...]

    def cross_wait(src, dst, ss, rs):
        def body(k, _):
            other = (z + k) % nz
            copy(src, dst(other), ss.at[k], rs.at[other], x * nz + c, (c + k) % nc).wait()
            return 0
        lax.fori_loop(1, nz, body, 0)

        @pl.when(c != z)
        def _():
            cross_copy(src, dst, ss, rs, 0).wait()

    for table in (own_tab, tmid, trp, tlp):
        table[owned:, :] = jnp.zeros((table.shape[0] - owned, LANES), F32)

    for load in loads[:4]:
        load.wait()
    for b in range(blocks):
        t = emb[b * LANES:(b + 1) * LANES, :].T
        sq_src[b:b + 1, :] = jnp.sum(t * t, axis=0, keepdims=True)
    cent_start(sq_src, sq_buf, sq_s, sq_r)
    zr[1, 1].start()
    zl[1, 0].start()
    xr[1, 1].start()
    xl[1, 0].start()

    ids = jnp.concatenate([cand[:, LANES * i:LANES * (i + 1)] for i in range(rows // LANES)], 0).astype(F32)
    qrows = ids.shape[0]
    owner = jnp.floor((ids + 0.5) * (1.0 / owned))
    loc = ids - owner * owned
    loc_top = jnp.floor(loc * (1.0 / LANES))
    loc_hi[...] = loc_top
    loc_lo[...] = loc - loc_top * LANES
    upper_ones = jnp.concatenate(
        [(iota((LANES, LANES), 0) < iota((LANES, LANES), 1)).astype(F32), jnp.ones((LANES, LANES), F32)],
        0).astype(BF16)
    lower = (iota((qrows, qrows), 0) > iota((qrows, qrows), 1)).astype(F32).astype(BF16)
    places = jnp.zeros((qrows, LANES), F32)
    for first in range(0, nd, 8):
        masks = [(owner == float(m)).astype(F32) for m in range(first, first + 8)]
        coded = [v.astype(BF16) for v in masks]
        above = jnp.dot(lower, jnp.concatenate(coded, 1), preferred_element_type=F32).astype(BF16)
        both = jnp.concatenate(
            [jnp.concatenate([coded[m], above[:, m * LANES:(m + 1) * LANES]], 1) for m in range(8)], 0)
        rank = jnp.dot(both, upper_ones, preferred_element_type=F32)
        for m in range(8):
            start = float((first + m) % nz * per_z + (first + m) // nz * per_owner)
            places = places + masks[m] * (rank[m * qrows:(m + 1) * qrows] + start)
    pos[...] = places
    top = jnp.floor(pos[...] * (1.0 / LANES))
    hi_ref[...] = top
    lo_ref[...] = pos[...] - top * LANES

    cent_wait(sq_src, sq_buf, sq_s, sq_r)
    total = sq_buf[0]
    for k in range(1, nc):
        total = total + sq_buf[k]
    alive = live_in[...].astype(F32)
    scale[...] = lax.rsqrt(total + 1e-6) * alive

    weights = jnp.concatenate([scale[...], jnp.zeros((LANES - blocks, LANES), F32)], 0).T
    for b in range(blocks):
        bsum[b:b + 1, :] = jnp.sum(
            weights[:, b:b + 1] * emb[b * LANES:(b + 1) * LANES, :], axis=0, keepdims=True)
    bcnt[...] = jnp.broadcast_to(jnp.sum(alive, axis=1, keepdims=True), (blocks, LANES))
    owners = [blk[b] // owned for b in range(blocks)]
    place_of = [jnp.int32(0)] + [
        jnp.where(owners[b] == owners[b - 1], 1, 0) for b in range(1, blocks)]
    local = [(blk[b] - owners[b] * owned).astype(F32) for b in range(blocks)]

    def message(i, _):
        line = iota((8, LANES), 0)
        tiles = [jnp.zeros((8, LANES), F32)] * 4
        for b in range(blocks):
            content = jnp.where(line < 2, bsum[b:b + 1, :], jnp.where(line < 4, local[b], bcnt[b:b + 1, :]))
            for k in range(4):
                at = jnp.where(owners[b] == i * 4 + k, place_of[b], 8)
                mine = (line == at) | (line == at + 2) | (line == at + 4)
                tiles[k] = jnp.where(mine, content, tiles[k])
        for k in range(4):
            msgs[i * 4 + k] = tiles[k]
        return 0

    lax.fori_loop(0, nd // 4, message, 0)

    def a2a_start(k, _):
        to = (me + k) % nd
        copy(msgs.at[to], rbuf.at[me], a2a_s.at[k], a2a_r.at[me], to, c).start()
        return 0

    def a2a_wait(k, _):
        other = (me + k) % nd
        copy(msgs.at[other], rbuf.at[other], a2a_s.at[k], a2a_r.at[other], other, c).wait()
        return 0

    lax.fori_loop(1, nd, a2a_start, 0)
    rbuf[me] = msgs[me]

    shift = (c * lrows).astype(F32)
    lane_row = iota((1, LANES), 1).astype(F32)

    def lists(i, acc):
        left_parts, right_parts = [], []
        for j in range(32):
            q = pl.ds(i * 32 + j, 1)
            at = (iota((lrows, LANES), 0).astype(F32) == hi_ref[q, :] - shift).astype(F32)
            left_parts.append(jnp.concatenate(
                [at * (i * 4 + j // 8).astype(F32), at * lane_row, at * loc_hi[q, :], at * loc_lo[q, :]], 0).astype(BF16))
            right_parts.append(
                (iota((LANES, LANES), 0).astype(F32) == lo_ref[q, :]).astype(F32).astype(BF16))
        return acc + lax.dot_general(
            jnp.concatenate(left_parts, 1), jnp.concatenate(right_parts, 1), NT, preferred_element_type=F32)

    found = lax.fori_loop(0, qrows // 32, lists, jnp.zeros((4 * lrows, LANES), F32))
    lsend[0] = (found[:lrows] * LANES + found[lrows:2 * lrows]).astype(I32)
    lsend[1] = (found[2 * lrows:3 * lrows] * LANES + found[3 * lrows:]).astype(I32)
    lists_at = lambda s: lbuf.at[s]
    cross_start(lsend, lists_at, l_s, l_r)

    forward(zr, zl, 1, 0)
    forward(xr, xl, 1, 0)
    forward(zr, zl, 1, 1)
    lax.fori_loop(1, nd, a2a_wait, 0)

    def slots(first, empty):
        return jnp.concatenate(
            [rbuf[:, first, :], rbuf[:, first + 1, :],
             jnp.full((LANES - 2 * nd, LANES), empty, F32)], 0)

    sums, slot_ids, slot_counts = slots(0, 0.0), slots(2, -1.0), slots(4, 0.0)
    slot_ids = jnp.where(slot_counts > 0, slot_ids, -1.0)
    ids_lane = slot_ids.T
    same = jnp.where((slot_ids == ids_lane) & (slot_counts > 0), 1.0, 0.0)
    group = jnp.dot(same.astype(BF16), jnp.concatenate(split3(sums), 1), preferred_element_type=F32)
    group = group[:, :LANES] + group[:, LANES:2 * LANES] + group[:, 2 * LANES:]
    square = group * group
    sq2_src[...] = jnp.broadcast_to(jnp.sum(square.T, axis=0, keepdims=True), (8, LANES))
    cent_start(sq2_src, sq2_buf, sq2_s, sq2_r)

    earlier = jnp.sum(
        jnp.where(iota((LANES, LANES), 0) < iota((LANES, LANES), 1), same, 0.0), axis=0, keepdims=True)
    first_ids = jnp.where(earlier > 0, -1.0, ids_lane[0:1])
    counts_lane = slot_counts.T[0:1]
    cent_wait(sq2_src, sq2_buf, sq2_s, sq2_r)
    total2 = sq2_buf[0]
    for k in range(1, nc):
        total2 = total2 + sq2_buf[k]
    inverse = lax.rsqrt(jnp.broadcast_to(total2[0:1], (LANES, LANES)) + 1e-6).T
    normal = group * inverse
    psend[0:SLOTS, :] = normal[:SLOTS]
    psend[SLOTS:SLOTS + 8, :] = jnp.broadcast_to(first_ids, (8, LANES))

    def patch_copy(k):
        return copy(psend, pbuf.at[k - 1], p_s.at[k - 1], p_r.at[k - 1], (x + k) % nx * nz + z, c)

    for k in range(1, nx):
        patch_copy(k).start()

    found_slots[0:SLOTS, :] = group[:SLOTS]
    found_slots[SLOTS:2 * SLOTS, :] = normal[:SLOTS]
    found_slots[2 * SLOTS:2 * SLOTS + 8, :] = jnp.broadcast_to(first_ids, (8, LANES))
    found_slots[2 * SLOTS + 8:2 * SLOTS + 16, :] = jnp.broadcast_to(ids_lane[0:1], (8, LANES))
    found_slots[2 * SLOTS + 16:2 * SLOTS + 24, :] = slot_counts.T[0:8]

    step = owned // 7
    rhs[...] = rhs_of(jnp.zeros((2 * LANES, LANES), BF16))

    def patch_rows(new, chosen, before, after):
        high, low = split2(new)
        rhs[0:SLOTS, 0:LANES] = high
        rhs[LANES:LANES + SLOTS, 0:LANES] = low

        def body(i, _):
            at = pl.ds(pl.multiple_of(i * step, 8), step)
            after[at, :] = replaced(chosen, rhs[...], i * step, before[at, :])
            return 0

        lax.fori_loop(0, 7, body, 0)

    loads[4].wait()
    patch_rows(normal[:SLOTS], first_ids, old, own_tab)

    cross_wait(lsend, lists_at, l_s, l_r)
    order = [0] + [d * s for d in range(1, nz // 2) for s in (-1, 1)] + [nz // 2]
    source = [(z + nz + d) % nz for d in order]
    for i in range(nz):
        here = pl.ds(i * lrows, lrows)
        pltpu.make_async_copy(lbuf.at[source[i], 0], srow.at[here], sm_sem.at[0, i]).start()
        pltpu.make_async_copy(lbuf.at[source[i], 1], sloc.at[here], sm_sem.at[1, i]).start()
    for i in range(nz):
        here = pl.ds(i * lrows, lrows)
        pltpu.make_async_copy(lbuf.at[source[i], 0], srow.at[here], sm_sem.at[0, i]).wait()
        pltpu.make_async_copy(lbuf.at[source[i], 1], sloc.at[here], sm_sem.at[1, i]).wait()

    documents = {0: emb, nz // 2: dmid}
    for d in range(1, nz // 2):
        documents[-d], documents[d] = dr[d - 1], dl[d - 1]
    tables = {0: own_tab, -1: trp, 1: tlp, 2: tmid}

    def dots(distance, dx):
        docs, table = documents[distance], tables[dx]
        first = order.index(distance) * lrows
        at = (x + nx + dx) % nx * urows

        def body(i, _):
            line = first + at + i
            for q in range(0, LANES, 8):
                stage[pl.ds(q, 8), :] = jnp.concatenate(
                    [docs[pl.ds(srow[line, u] & (rows - 1), 1), :]
                     * table[pl.ds(sloc[line, u] & (table.shape[0] - 1), 1), :]
                     for u in range(q, q + 8)], 0)
            part[pl.ds(line, 1), :] = jnp.sum(stage[...].T, axis=0, keepdims=True)
            return 0

        lax.fori_loop(0, urows, body, 0)

    def part_copy(i):
        return copy(part.at[pl.ds(i * lrows, lrows)], s1buf.at[c], s1_s.at[i], s1_r.at[c], me, source[i])

    def hand_on(distance):
        i = order.index(distance)

        @pl.when(source[i] != c)
        def _():
            part_copy(i).start()

        @pl.when(source[i] == c)
        def _():
            s1buf[c] = part[pl.ds(i * lrows, lrows), :]

    def patch(k, before, after):
        patch_copy(k).wait_recv()
        new = pbuf[k - 1]
        patch_rows(new[:SLOTS], new[SLOTS:SLOTS + 1], before, after)

    for d in (0, -1, 1):
        dots(d, 0)
    forward(zr, zl, 2, 0)
    xr[1, 1].wait_recv()
    xl[1, 0].wait_recv()
    patch(1, tr[0], trp)
    patch(3, tl[0], tlp)
    for d in (0, -1, 1):
        dots(d, -1)
        dots(d, 1)
    forward(zr, zl, 2, 1)
    for d in (-2, 2):
        for dx in (0, -1, 1):
            dots(d, dx)
    forward(zr, zl, 3, 0)
    xr[2, 0].wait_recv()
    xl[2, 1].wait_recv()
    patch(2, tmid, tmid)
    for d in (0, -1, 1, -2, 2):
        dots(d, 2)
        hand_on(d)
    forward(zr, zl, 3, 1)
    for d in (-3, 3):
        for dx in (0, -1, 1, 2):
            dots(d, dx)
        hand_on(d)
    share = qrows // nc
    tops = []
    for g in range(share // 8):
        own = [pl.ds(c * share + g * 8 + j, 1) for j in range(8)]
        sel[:, g * 8 * LANES:(g + 1) * 8 * LANES] = jnp.concatenate(
            [(iota((LANES, LANES), 0).astype(F32) == lo_ref[v, :]).astype(F32).astype(BF16) for v in own], 1)
        tops.append(jnp.concatenate([hi_ref[v, :] for v in own], 1))
    sums_at = lambda s: tbuf.at[pl.ds(pl.multiple_of(s * lrows, 8), lrows)]

    @pl.when(c != facing)
    def _():
        def part_wait(k, _):
            other = (c + k) % nc
            copy(full, s1buf.at[other], s1_s.at[0], s1_r.at[other], me, other).wait_recv()
            return 0

        lax.fori_loop(1, nc, part_wait, 0)
        total3 = s1buf[0]
        for k in range(1, nc):
            total3 = total3 + s1buf[k]
        full[...] = total3
        cross_start(full, sums_at, t_s, t_r)

    zr[4, 0].wait_recv()
    zl[4, 1].wait_recv()
    for dx in (0, -1, 1, 2):
        dots(4, dx)
    last = order.index(nz // 2)

    def facing_copy(k):
        other = (c + k) % nc
        return copy(part.at[pl.ds(last * lrows, lrows)], obuf.at[c], o_s.at[k], o_r.at[c], x * nz + facing, other)

    lax.fori_loop(0, nc, lambda k, _: (facing_copy(k).start(), 0)[1], 0)

    def sums_copy(s):
        return copy(full, sums_at(s), t_s.at[0], t_r.at[s], x * nz + c, (c + 1) % nc)

    for k in range(1, nz):
        if k != nz // 2:
            sums_copy((z + k) % nz).wait_recv()

    @pl.when(c != z)
    def _():
        sums_copy(z).wait_recv()

    def facing_wait(k, _):
        other = (c + k) % nc
        copy(full, obuf.at[other], o_s.at[k], o_r.at[other], x * nz + facing, other).wait_recv()
        return 0

    lax.fori_loop(0, nc, facing_wait, 0)
    total4 = obuf[0]
    for k in range(1, nc):
        total4 = total4 + obuf[k]
    tbuf[pl.ds(pl.multiple_of(facing * lrows, 8), lrows), :] = total4

    table = jnp.concatenate(split2(tbuf[...]), 0)
    for g in range(share // 8):
        got = jnp.dot(table, sel[:, g * 8 * LANES:(g + 1) * 8 * LANES], preferred_element_type=F32)
        got = got[:qrows] + got[qrows:]
        line = jnp.sum(
            jnp.where(iota(got.shape, 0).astype(F32) == tops[g], got, 0.0), axis=0, keepdims=True)
        factor = scale[pl.ds(c * (share // 8) + g, 1), :]
        for j in range(8):
            cos[j:j + 1, g * LANES:(g + 1) * LANES] = line[:, j * LANES:(j + 1) * LANES] * factor

    for ring_copies in (zr, zl, xr, xl):
        for one in ring_copies.values():
            one.wait_send()
    for k in range(1, nx):
        patch_copy(k).wait_send()
    for i in range(nz):
        if i != last:
            @pl.when(source[i] != c)
            def _(i=i):
                part_copy(i).wait_send()

    lax.fori_loop(0, nc, lambda k, _: (facing_copy(k).wait_send(), 0)[1], 0)

    @pl.when(c != facing)
    def _():
        lax.fori_loop(1, nc, lambda k, _: (cross_copy(full, sums_at, t_s, t_r, k).wait_send(), 0)[1], 0)

        @pl.when(c != z)
        def _():
            cross_copy(full, sums_at, t_s, t_r, 0).wait_send()


def on_device(nd, nc, embeddings, row_mask, block_cluster, candidates, old_centroids):
    rows, width = embeddings.shape
    owned = old_centroids.shape[0]
    nz = Z_CHIPS
    nx = nd // nz
    cands = candidates.shape[1]
    blocks = block_cluster.shape[0]
    qrows = rows * cands // LANES
    lrows = qrows // nz
    table_rows = 1 << (owned - 1).bit_length()
    vmem = lambda *s: pltpu.VMEM(s, F32)
    dma = lambda *s: pltpu.SemaphoreType.DMA(s)
    in_vmem = pl.BlockSpec(memory_space=pltpu.VMEM)
    scratch = [
        vmem(rows, width), vmem(owned, width), pltpu.VMEM((blocks, LANES), I32), pltpu.VMEM((cands, rows), I32),
        pltpu.SMEM((blocks,), I32),
        [vmem(rows, width)] * (nz // 2 - 1), [vmem(rows, width)] * (nz // 2 - 1), vmem(rows, width),
        [vmem(owned, width)], [vmem(owned, width)], *[vmem(table_rows, width)] * 4,
        vmem(blocks, LANES), vmem(nc, blocks, LANES), vmem(blocks, LANES),
        vmem(blocks, LANES), vmem(blocks, LANES),
        vmem(qrows, LANES), vmem(qrows, LANES), vmem(qrows, LANES), vmem(qrows, LANES), vmem(qrows, LANES),
        vmem(nd, 8, LANES), vmem(nd, 8, LANES), vmem(8, LANES), vmem(nc, 8, LANES),
        pltpu.VMEM((2 * LANES, 2 * LANES), BF16), vmem(SLOTS + 8, LANES), vmem(nx - 1, SLOTS + 8, LANES),
        pltpu.VMEM((2, lrows, LANES), I32), pltpu.VMEM((nz, 2, lrows, LANES), I32),
        pltpu.SMEM((qrows, LANES), I32), pltpu.SMEM((qrows, LANES), I32),
        vmem(LANES, LANES), vmem(qrows, LANES), vmem(nc, lrows, LANES), vmem(lrows, LANES), vmem(qrows, LANES),
        pltpu.VMEM((LANES, rows * cands // nc), BF16), vmem(nc, lrows, LANES),
        dma(nz // 2, 2), dma(nz // 2, 2), dma(nz // 2, 2), dma(nz // 2, 2),
        dma(nx // 2, 2), dma(nx // 2, 2), dma(nx // 2, 2), dma(nx // 2, 2),
        dma(nc), dma(nc), dma(nc), dma(nc), dma(nd), dma(nd), dma(nx - 1), dma(nx - 1),
        dma(nc), dma(nz), dma(2, nz), dma(nz), dma(nc), dma(nc), dma(nz), dma(5), dma(nc), dma(nc),
    ]
    slots, cosines = pl.pallas_call(
        functools.partial(kernel, nd, nz, nc),
        out_shape=(
            jax.ShapeDtypeStruct((2 * SLOTS + 24, width), F32),
            jax.ShapeDtypeStruct((cands, rows // nc), F32),
        ),
        in_specs=[pl.BlockSpec(memory_space=pltpu.HBM)] * 5,
        out_specs=(in_vmem,) * 2,
        scratch_shapes=scratch,
        compiler_params=pltpu.CompilerParams(
            collective_id=0, has_side_effects=True, vmem_limit_bytes=65536 * 1000),
        name="update",
    )(embeddings, old_centroids, row_mask.reshape(blocks, rows // blocks), candidates.T, block_cluster)
    steps = 4
    step = owned // steps
    table_block = pl.BlockSpec((step, width), lambda i: (i, 0))
    whole = lambda shape: pl.BlockSpec(shape, lambda i: (0, 0))
    counts_shape = (-(-owned // (8 * LANES)) * 8, LANES)
    sums, counts, cents = pl.pallas_call(
        expand,
        grid=(steps,),
        out_shape=(
            jax.ShapeDtypeStruct((owned, width), F32),
            jax.ShapeDtypeStruct(counts_shape, I32),
            jax.ShapeDtypeStruct((owned, width), F32),
        ),
        in_specs=[whole(slots.shape), table_block],
        out_specs=(table_block, whole(counts_shape), table_block),
        compiler_params=pltpu.CompilerParams(vmem_limit_bytes=16 << 20),
        name="expand",
    )(slots, old_centroids)
    return sums, counts.reshape(-1)[:owned], cents, cosines.T


def solution(mesh):
    placed = (P("doc", "cent"), P("doc"), P("doc"), P("doc", None), P("doc", "cent"))
    return jax.shard_map(
        functools.partial(on_device, mesh.shape["doc"], mesh.shape["cent"]),
        mesh=mesh,
        in_specs=placed,
        out_specs=(P("doc", "cent"), P("doc"), P("doc", "cent"), P(("doc", "cent"), None)),
        check_vma=False,
    )
```
